256 devices in a mesh: section: 16 (over y, x), dp: 16 (over z, core).
Axes of the slice: x: 4, y: 4, z: 8, core: 2. Of those that a mesh axis runs over, the one named last changes fastest.
Arguments:
- hidden_acts: bfloat16 [16, 2048, 28672], P('section', 'dp'), may hold values from -6 to 6
- resid_stream: bfloat16 [16, 2048, 8192], P('section', 'dp'), may hold values from -6 to 6
- norm_scale: float32 [16, 8192], P('section'), may hold values from -1 to 1
- out_grad: bfloat16 [2048, 8192], P('dp'), may hold values from -6 to 6
- lengths: int32 [32], P('dp'), may hold values from 1 to 64, 1792 in all
- proj_in: bfloat16 [16, 64, 28672], P('section'), may hold values from -0.03125 to 0.03125
- proj_out: bfloat16 [16, 64, 8192], P('section'), may hold values from -0.0625 to 0.0625
- queries: bfloat16 [16, 512, 4096], P('section', 'dp'), may hold values from -0.09375 to 0.09375
Outputs:
- scores: float32 [32, 512], P(None, 'dp')
- in_grads: bfloat16 [16, 2048, 8192], P('section', 'dp')
The draws below stay inside these ranges and needn't reach their ends.
Inputs may be any that keep to these rules, and one draw needn't show every extreme that they name: Some sequence has exactly 64 live tokens; the lengths sum to 1792.
All inputs are finite; a program needn't handle non-finite values. No bound on the sum of `lengths` on one device may be relied on, other than what follows from the above.
Results may differ from the reference program's by a relative error of at most 0.012.
Values may be sent and summed in bfloat16 or wider, within the bound.
No kernel may reach another device: no remote copies, remote signals or barrier semaphores. Data moves between devices by JAX's collectives and lax.ppermute only.
A program may use at most 64 MiB of HBM per device.

```python
import math
import jax
import jax.numpy as jnp
import numpy as np
from jax import lax

D = 8192
FF = 28672
RANK = 64
QUERIES = 512
LEN = 64
EXAMPLES = 32
TOKENS = 2048
N_SECTION = 16


def shard_levels(key, dims, split, smallest, top_value):
    def one(position, shards_of):
        steps = jax.random.uniform(jax.random.fold_in(jax.random.fold_in(key, 6), position), (shards_of,), jnp.float32, smallest / len(split), top_value / len(split))
        return jnp.repeat(jnp.exp(steps), dims[position] // shards_of).reshape((-1,) + (1,) * (len(dims) - position - 1))

    gain = one(*split[0])
    for cut in split[1:]:
        gain = gain * one(*cut)
    return gain


def length_profile(number_of, total, most, skew):
    weights = [(1 << 20) // math.isqrt(grade ** skew) + 1 for grade in range(2, number_of + 1)]
    rest, given = total - most - (number_of - 1), [1] * (number_of - 1)
    while rest > 0:
        free = [i for i in range(number_of - 1) if given[i] < most]
        mass, budget = sum([weights[i] for i in free]), rest
        for i in free:
            more = min(most - given[i], max(1, budget * weights[i] // mass), rest)
            given[i] = given[i] + more
            rest = rest - more
    return np.array([most] + given)


def uneven_parts(stream_key, count, total, reach, lean):
    if count == 2:
        one = jax.random.randint(stream_key, (), max(1, total - reach), min(reach, total - 1) + 1)
        return jnp.stack([one, total - one])
    sizes = jnp.asarray(length_profile(count, total, reach, lean), jnp.int32)
    twos = (count - 1) // 2
    giver, taker = sizes[1:1 + 2 * twos:2], sizes[2:2 + 2 * twos:2]
    room = jnp.minimum(giver - 1, reach - taker)
    moved = jax.random.randint(jax.random.fold_in(stream_key, 1), (twos,), 0, 1 << 20) % (room + 1)
    sizes = sizes.at[1:1 + 2 * twos:2].set(giver - moved).at[2:2 + 2 * twos:2].set(taker + moved)
    return sizes[jax.random.permutation(jax.random.fold_in(stream_key, 2), count)]


def noise(rng, extent, scale, bound, split=(), kind=jnp.bfloat16):
    drawn = jax.random.normal(rng, extent, jnp.float32) * scale
    if len(split) > 0:
        drawn = shard_levels(rng, extent, split, -0.22, 0.18) * drawn
    return jnp.clip(drawn, min=-bound, max=bound).astype(kind)


def setup_inputs(seed: int = 0) -> dict:
    seeds = jax.random.split(jax.random.key(seed), 9)
    return {
        "hidden_acts": noise(seeds[0], (N_SECTION, TOKENS, FF), 1.0, 6.0, ((0, 16), (1, 16))),
        "resid_stream": noise(seeds[1], (N_SECTION, TOKENS, D), 1.0, 6.0, ((0, 16), (1, 16))),
        "norm_scale": jnp.clip(jax.random.uniform(seeds[2], (N_SECTION, D), jnp.float32, -1.0, 1.0) * shard_levels(seeds[2], (N_SECTION, D), ((0, 16),), -0.4, 0.0), -1.0, 1.0),
        "out_grad": noise(seeds[3], (TOKENS, D), 1.0, 6.0, ((0, 16),)),
        "lengths": uneven_parts(seeds[4], EXAMPLES, EXAMPLES * LEN * 7 // 8, LEN, 1).astype(jnp.int32),
        "proj_in": noise(seeds[5], (N_SECTION, RANK, FF), FF ** -0.5, 0.03125, ((0, 16),)),
        "proj_out": noise(seeds[6], (N_SECTION, RANK, D), D ** -0.5, 0.0625, ((0, 16),)),
        "queries": noise(seeds[7], (N_SECTION, QUERIES, RANK * RANK), (RANK * RANK) ** -0.5, 0.09375, ((0, 16), (1, 16))),
    }


def chain_back(grad_rows, resid_rows, norm_gain):
    grad_f32 = grad_rows.astype(jnp.float32)
    resid_f32 = resid_rows.astype(jnp.float32)
    inv_rms = lax.rsqrt(lax.optimization_barrier(jnp.mean(resid_f32 * resid_f32, axis=-1, keepdims=True)) + 1e-05)
    weighted = grad_f32 * norm_gain
    inner_mean = lax.optimization_barrier(jnp.mean(weighted * resid_f32, axis=-1, keepdims=True))
    result = grad_f32 + inv_rms * weighted - resid_f32 * (inv_rms * inv_rms * inv_rms) * inner_mean
    return result.astype(jnp.bfloat16)

def project(hidden_rows, grad_rows, weight_in, weight_out):
    side_in = jnp.dot(hidden_rows, weight_in.T, preferred_element_type=jnp.float32).astype(jnp.bfloat16)
    side_out = jnp.dot(grad_rows, weight_out.T, preferred_element_type=jnp.float32).astype(jnp.bfloat16)
    side_in = side_in.reshape(EXAMPLES, LEN, RANK).astype(jnp.float32)
    side_out = side_out.reshape(EXAMPLES, LEN, RANK).astype(jnp.float32)
    outer = jnp.einsum('eto,eti->eoi', side_out, side_in)
    return outer.reshape(EXAMPLES, RANK * RANK).astype(jnp.bfloat16)

def reference(hidden_acts, resid_stream, norm_scale, out_grad, lengths, proj_in, proj_out, queries):
    positions = jnp.arange(LEN, dtype=jnp.int32)
    live_mask = (positions[None, :] < lengths[:, None]).reshape(TOKENS, 1)
    grad_rows = jnp.where(live_mask, out_grad, jnp.zeros_like(out_grad))
    raw = jnp.zeros((EXAMPLES, QUERIES), jnp.float32)
    squares = jnp.zeros((EXAMPLES,), jnp.float32)
    collected = []
    for section_num in range(N_SECTION - 1, -1, -1):
        example_grads = project(hidden_acts[section_num], grad_rows, proj_in[section_num], proj_out[section_num])
        raw = raw + jnp.dot(example_grads, queries[section_num].T, preferred_element_type=jnp.float32)
        grads_f32 = example_grads.astype(jnp.float32)
        squares = squares + lax.optimization_barrier(jnp.sum(grads_f32 * grads_f32, axis=1))
        grad_rows = chain_back(grad_rows, resid_stream[section_num], norm_scale[section_num])
        collected.append(grad_rows)
    in_grads = jnp.stack(collected[::-1], axis=0)
    scores = raw / jnp.sqrt(squares / (N_SECTION * RANK * RANK) + 1e-06)[:, None]
    return (scores, in_grads)
```

```python
import jax
import jax.numpy as jnp
from jax import lax
from jax.experimental import pallas as pl
from jax.experimental.pallas import tpu as pltpu
from jax.sharding import PartitionSpec as P

EPS = 1e-05
LANES = 128
SUBLANES = 16


def chain_kernel(recv_ref, top_ref, out_ref, gain_ref, *, sections, width, lanes_per):
    blocks = top_ref.shape[0]
    gain_blocks = gain_ref.shape[0] // SUBLANES
    step = 4
    chunks = blocks // step
    out_ref[sections - 1] = top_ref[...]

    def one(turn, _):
        s = sections - 1 - turn
        hi = recv_ref[s, pl.ds(blocks, gain_blocks)].astype(jnp.float32)
        lo = recv_ref[s, pl.ds(blocks + gain_blocks, gain_blocks)].astype(jnp.float32)
        gain_ref[...] = (hi + lo).reshape(gain_blocks * SUBLANES, LANES)

        def gain_of(k):
            return jnp.stack(
                [
                    jnp.concatenate(
                        [
                            jnp.broadcast_to(gain_ref[pl.ds(2 * i, 1), :], (8, LANES)),
                            jnp.broadcast_to(gain_ref[pl.ds(2 * i + 1, 1), :], (8, LANES)),
                        ],
                        axis=0,
                    )
                    for i in range(k * step, (k + 1) * step)
                ]
            )

        square = jnp.zeros((step, SUBLANES, LANES), jnp.float32)
        inner = jnp.zeros((step, SUBLANES, LANES), jnp.float32)
        for k in range(chunks):
            x = recv_ref[s, pl.ds(k * step, step)].astype(jnp.float32)
            g = out_ref[s, pl.ds(k * step, step)].astype(jnp.float32)
            square = square + x * x
            inner = inner + g * gain_of(k) * x

        def total(v):
            v = jnp.sum(v, axis=0)
            v = v[:8] + v[8:]
            v = jnp.sum(v, axis=-1, keepdims=True)
            return jnp.concatenate([v, v], axis=0)[None]

        inv = lax.rsqrt(total(square) / width + EPS)
        pull = inv * inv * inv * (total(inner) / width)
        for k in range(chunks):
            x = recv_ref[s, pl.ds(k * step, step)].astype(jnp.float32)
            g = out_ref[s, pl.ds(k * step, step)].astype(jnp.float32)
            new = g + inv * (g * gain_of(k)) - x * pull
            out_ref[s - 1, pl.ds(k * step, step)] = new.astype(jnp.bfloat16)
        return 0

    lax.fori_loop(0, sections - 1, one, 0)


def chain_all(recv, top):
    sections = recv.shape[0]
    blocks = top.shape[0]
    gain_blocks = (recv.shape[1] - blocks) // 2
    width = blocks * 2 * LANES

    def body(recv_ref, top_ref, out_ref, gain_ref):
        chain_kernel(recv_ref, top_ref, out_ref, gain_ref, sections=sections, width=width, lanes_per=LANES)

    return pl.pallas_call(
        body,
        out_shape=jax.ShapeDtypeStruct((sections, blocks, SUBLANES, LANES), jnp.bfloat16),
        in_specs=[pl.BlockSpec(memory_space=pltpu.VMEM)] * 2,
        out_specs=pl.BlockSpec(memory_space=pltpu.VMEM),
        scratch_shapes=[pltpu.VMEM((gain_blocks * SUBLANES, LANES), jnp.float32)],
        compiler_params=pltpu.CompilerParams(vmem_limit_bytes=24 * 1024 * 1024),
        name="chain_all",
    )(recv, top)


def to_tiles(rows):
    count, width = rows.shape
    tiles = rows.reshape(count // 8, 8, width // LANES, LANES).transpose(0, 2, 1, 3)
    return tiles.reshape(count // 8, width // (2 * LANES), SUBLANES, LANES)


def from_tiles(tiles):
    groups, blocks = tiles.shape[:2]
    rows = tiles.reshape(groups, blocks * 2, 8, LANES).transpose(0, 2, 1, 3)
    return rows.reshape(groups * 8, blocks * 2 * LANES)


def chain_back(grad_rows, resid_rows, norm_gain):
    grad_f32 = grad_rows.astype(jnp.float32)
    resid_f32 = resid_rows.astype(jnp.float32)
    inv_rms = lax.rsqrt(jnp.mean(resid_f32 * resid_f32, axis=-1, keepdims=True) + EPS)
    weighted = grad_f32 * norm_gain
    inner_mean = jnp.mean(weighted * resid_f32, axis=-1, keepdims=True)
    result = grad_f32 + inv_rms * weighted - resid_f32 * (inv_rms * inv_rms * inv_rms) * inner_mean
    return result.astype(jnp.bfloat16)


def shards(hidden_acts, resid_stream, norm_scale, out_grad, lengths, proj_in, proj_out, queries):
    tok_rows, features = out_grad.shape
    examples = lengths.shape[0]
    seq_len = tok_rows // examples
    rank_size = proj_in.shape[1]
    sections = lax.axis_size("section")
    ranks = lax.axis_size("dp")
    me = lax.axis_index("section")
    resid_rows = resid_stream[0]
    norm_gain = norm_scale[0]

    own = tok_rows // sections
    gain_hi = lax.reduce_precision(norm_gain, 8, 7)
    gain_halves = jnp.concatenate([gain_hi, norm_gain - gain_hi]).astype(jnp.bfloat16)
    gain_tiles = gain_halves.reshape(-1, SUBLANES, LANES)
    send = jnp.concatenate(
        [to_tiles(resid_rows), jnp.broadcast_to(gain_tiles[None], (sections,) + gain_tiles.shape)], axis=1
    )
    recv = lax.all_to_all(send, "section", 0, 0)

    own_rows = lax.dynamic_slice_in_dim(out_grad, me * own, own, axis=0)
    own_slots = me * own + jnp.arange(own, dtype=jnp.int32)
    own_live = own_slots % seq_len < jnp.take(lengths, own_slots // seq_len)
    own_top = jnp.where(own_live[:, None], own_rows, jnp.zeros_like(own_rows))
    grads = chain_all(recv, to_tiles(own_top)[0])
    held_grad = from_tiles(lax.all_to_all(grads, "section", 0, 0))

    side_in = jnp.einsum(
        "tf,rf->tr", hidden_acts[0], proj_in[0], preferred_element_type=jnp.float32
    ).astype(jnp.bfloat16)
    side_out = jnp.einsum(
        "td,rd->tr", held_grad, proj_out[0], preferred_element_type=jnp.float32
    ).astype(jnp.bfloat16)
    in_grad = chain_back(held_grad, resid_rows, norm_gain)
    outer = jnp.einsum(
        "eto,eti->eoi",
        side_out.reshape(examples, seq_len, rank_size),
        side_in.reshape(examples, seq_len, rank_size),
        preferred_element_type=jnp.float32,
    )
    example_grads = outer.reshape(examples, rank_size * rank_size).astype(jnp.bfloat16)
    spread = jnp.broadcast_to(example_grads[None], (ranks,) + example_grads.shape)
    gathered = lax.all_to_all(spread, "dp", 0, 0).reshape(ranks * examples, rank_size * rank_size)
    partial_value = jnp.einsum(
        "ek,qk->eq", gathered, queries[0], preferred_element_type=jnp.float32
    )
    grads_f32 = gathered.astype(jnp.float32)
    squares = jnp.sum(grads_f32 * grads_f32, axis=1, keepdims=True)
    both = jnp.concatenate([partial_value, squares], axis=1)
    parts = lax.all_to_all(jnp.broadcast_to(both[None], (sections,) + both.shape), "section", 0, 0)
    summed = jnp.sum(parts, axis=0)
    scores = summed[:, :-1] / jnp.sqrt(summed[:, -1:] / (sections * rank_size * rank_size) + 1e-06)
    return (scores, in_grad[None])


def solution(mesh):
    in_specs = (
        P("section", "dp", None),
        P("section", "dp", None),
        P("section", None),
        P("dp", None),
        P("dp"),
        P("section", None, None),
        P("section", None, None),
        P("section", "dp", None),
    )
    out_specs = (P(None, "dp"), P("section", "dp", None))
    return jax.shard_map(shards, mesh=mesh, in_specs=in_specs, out_specs=out_specs, check_vma=False)
```

```python
import functools
import math

import jax
import jax.numpy as jnp
from jax import lax
from jax.experimental import pallas as pl
from jax.experimental.pallas import tpu as pltpu
from jax.sharding import PartitionSpec as P

EPS = 1e-05
LANES = 128
SUBLANES = 16


def chain_kernel(place_ref, recv_ref, top_ref, *refs):
    *near_refs, out_ref, gain_ref, grad_ref, kept_ref, inv_ref, out_sem = refs
    sections, blocks = recv_ref.shape[:2]
    side = len(near_refs)
    width = blocks * 2 * LANES
    step = 4
    chunks = blocks // step
    row, column = place_ref[0] // side, place_ref[0] % side

    def leaving(group):
        span = pl.ds(group * side, side)
        return pltpu.make_async_copy(grad_ref.at[span], out_ref.at[span], out_sem.at[group])

    for down in range(side):
        for across in range(side):
            s = (row + side - down) % side * side + (column + side - across) % side
            gain_ref[s] = near_refs[down][across]
    grad_ref[sections - 1] = top_ref[...]

    def gain_of(s, k):
        return jnp.stack(
            [
                jnp.concatenate(
                    [
                        jnp.broadcast_to(gain_ref[s, pl.ds(2 * i, 1), :], (8, LANES)),
                        jnp.broadcast_to(gain_ref[s, pl.ds(2 * i + 1, 1), :], (8, LANES)),
                    ],
                    axis=0,
                )
                for i in range(k * step, (k + 1) * step)
            ]
        )

    def span(k):
        return pl.ds(k * step, step)

    def mean(v):
        v = jnp.sum(v, axis=0)
        v = v[:8] + v[8:]
        v = jnp.sum(v, axis=-1, keepdims=True) / width
        return jnp.broadcast_to(jnp.concatenate([v, v], axis=0), (SUBLANES, LANES))

    zero = jnp.zeros((step, SUBLANES, LANES), jnp.float32)
    for s in range(sections - 1, 0, -1):
        square = zero
        for k in range(chunks):
            x = recv_ref[s, span(k)].astype(jnp.float32)
            square = square + x * x
        inv_ref[s] = lax.rsqrt(mean(square) + EPS)

    def enter(s, k, g, inner):
        weighted = g * gain_of(s, k)
        kept_ref[span(k)] = g + inv_ref[s][None] * weighted
        return inner + weighted * recv_ref[s, span(k)].astype(jnp.float32)

    inner = zero
    for k in range(chunks):
        inner = enter(sections - 1, k, grad_ref[sections - 1, span(k)].astype(jnp.float32), inner)
    for s in range(sections - 1, 0, -1):
        inv = inv_ref[s]
        pull = (inv * inv * inv * mean(inner))[None]
        inner = zero
        for k in range(chunks):
            new = kept_ref[span(k)] - recv_ref[s, span(k)].astype(jnp.float32) * pull
            new = new.astype(jnp.bfloat16)
            grad_ref[s - 1, span(k)] = new
            if s > 1:
                inner = enter(s - 1, k, new.astype(jnp.float32), inner)
        if (s - 1) % side == 0:
            leaving((s - 1) // side).start()
    for group in range(side):
        leaving(group).wait()


def in_vmem(body, out_shape, name, scalars=0, scratch=()):
    def call(*args):
        specs = [pl.BlockSpec(memory_space=pltpu.SMEM)] * scalars
        specs += [pl.BlockSpec(memory_space=pltpu.VMEM)] * (len(args) - scalars)
        return pl.pallas_call(
            body,
            out_shape=out_shape,
            in_specs=specs,
            out_specs=pl.BlockSpec(memory_space=pltpu.VMEM),
            scratch_shapes=list(scratch),
            compiler_params=pltpu.CompilerParams(vmem_limit_bytes=24 * 1024 * 1024),
            name=name,
        )(*args)

    return call


def chain_all(place, recv, top, near):
    sections, blocks = recv.shape[:2]
    shape = (sections, blocks, SUBLANES, LANES)
    side = len(near)
    return pl.pallas_call(
        chain_kernel,
        out_shape=pltpu.HBM(shape, jnp.bfloat16),
        in_specs=[pl.BlockSpec(memory_space=pltpu.SMEM)] + [pl.BlockSpec(memory_space=pltpu.VMEM)] * (2 + side),
        out_specs=pl.BlockSpec(memory_space=pltpu.HBM),
        scratch_shapes=[
            pltpu.VMEM((sections, 2 * blocks, LANES), jnp.float32),
            pltpu.VMEM(shape, jnp.bfloat16),
            pltpu.VMEM(shape[1:], jnp.float32),
            pltpu.VMEM((sections, SUBLANES, LANES), jnp.float32),
            pltpu.SemaphoreType.DMA((side,)),
        ],
        compiler_params=pltpu.CompilerParams(vmem_limit_bytes=16 * 1024 * 1024),
        name="chain_all",
    )(place, recv, top, *near)


def front_kernel(held_ref, weight_ref, side_in_ref, out_ref):
    side_out = lax.dot_general(
        held_ref[...], weight_ref[...], (((1,), (1,)), ((), ())), preferred_element_type=jnp.float32
    ).astype(jnp.bfloat16)
    examples = out_ref.shape[0]
    rows = side_out.shape[0] // examples
    for e in range(examples):
        out_ref[e] = lax.dot_general(
            side_out[e * rows : (e + 1) * rows],
            side_in_ref[pl.ds(e * rows, rows), :],
            (((0,), (0,)), ((), ())),
            preferred_element_type=jnp.float32,
        ).astype(jnp.bfloat16)


def raw_kernel(grads_ref, queries_ref, out_ref):
    grads = grads_ref[...]
    share = queries_ref.shape[0]
    raw = lax.dot_general(
        grads, queries_ref[...], (((1,), (1,)), ((), ())), preferred_element_type=jnp.float32
    )
    wide = grads.astype(jnp.float32)
    squares = jnp.broadcast_to(jnp.sum(wide * wide, axis=1, keepdims=True), raw.shape)

    def folded(v):
        return jnp.concatenate([v[8 * j : 8 * j + 8] for j in range(v.shape[0] // 8)], axis=1)

    block = jnp.concatenate([folded(raw), folded(squares)], axis=0)
    for s in range(out_ref.shape[0]):
        out_ref[s] = block


def scores_kernel(parts_ref, out_ref, *, count):
    total = parts_ref[0]
    for s in range(1, parts_ref.shape[0]):
        total = total + parts_ref[s]
    scores = total[:8] / jnp.sqrt(total[8:] / count + 1e-06)
    share = out_ref.shape[1]
    for j in range(out_ref.shape[0] // 8):
        out_ref[pl.ds(8 * j, 8), :] = scores[:, j * share : (j + 1) * share]


def to_tiles(rows):
    count, width = rows.shape
    tiles = rows.reshape(count // 8, 8, width // LANES, LANES).transpose(0, 2, 1, 3)
    return tiles.reshape(count // 8, width // (2 * LANES), SUBLANES, LANES)


def from_tiles(tiles):
    groups, blocks = tiles.shape[:2]
    rows = tiles.reshape(groups, blocks * 2, 8, LANES).transpose(0, 2, 1, 3)
    return rows.reshape(groups * 8, blocks * 2 * LANES)


def chain_back(grad_rows, resid_rows, norm_gain):
    grad_f32 = grad_rows.astype(jnp.float32)
    resid_f32 = resid_rows.astype(jnp.float32)
    inv_rms = lax.rsqrt(jnp.mean(resid_f32 * resid_f32, axis=-1, keepdims=True) + EPS)
    weighted = grad_f32 * norm_gain
    inner_mean = jnp.mean(weighted * resid_f32, axis=-1, keepdims=True)
    result = grad_f32 + inv_rms * weighted - resid_f32 * (inv_rms * inv_rms * inv_rms) * inner_mean
    return result.astype(jnp.bfloat16)


def shards(hidden_acts, resid_stream, norm_scale, out_grad, lengths, proj_in, proj_out, queries):
    tok_rows, features = out_grad.shape
    examples = lengths.shape[0]
    seq_len = tok_rows // examples
    rank_size = proj_in.shape[1]
    sections = lax.axis_size("section")
    ranks = lax.axis_size("dp")
    share = queries.shape[1]
    me = lax.axis_index("section")
    resid_rows = resid_stream[0]
    norm_gain = norm_scale[0]

    side = math.isqrt(sections)
    grid = [(row, column) for row in range(side) for column in range(side)]

    def moved(value, down, across):
        pairs = [
            (row * side + column, (row + down) % side * side + (column + across) % side) for row, column in grid
        ]
        return lax.ppermute(value, "section", pairs)

    gain_tiles = norm_gain.reshape(-1, LANES)
    across = [moved(gain_tiles, 0, k) for k in range(1, side)]
    resid_first, across[0] = lax.optimization_barrier((resid_rows, across[0]))
    near = [jnp.stack([gain_tiles] + across)]
    near += [moved(near[0], k, 0) for k in range(1, side)]

    own = tok_rows // sections
    recv = lax.all_to_all(to_tiles(resid_first), "section", 0, 0)
    own_rows = lax.dynamic_slice_in_dim(out_grad, me * own, own, axis=0)
    own_slots = me * own + jnp.arange(own, dtype=jnp.int32)
    own_live = own_slots % seq_len < jnp.take(lengths, own_slots // seq_len)
    own_top = jnp.where(own_live[:, None], own_rows, jnp.zeros_like(own_rows))
    grads = chain_all(me.astype(jnp.int32).reshape(1), recv, to_tiles(own_top)[0], near)
    held_grad = from_tiles(lax.all_to_all(grads, "section", 0, 0))

    side_in = jnp.einsum(
        "tf,rf->tr", hidden_acts[0], proj_in[0], preferred_element_type=jnp.float32
    ).astype(jnp.bfloat16)
    in_grad = chain_back(held_grad, resid_rows, norm_gain)
    outer = in_vmem(front_kernel, jax.ShapeDtypeStruct((examples, rank_size, rank_size), jnp.bfloat16), "front")(
        held_grad, proj_out[0], side_in
    )
    example_grads = outer.reshape(examples, rank_size * rank_size)
    spread = jnp.broadcast_to(example_grads[None], (ranks,) + example_grads.shape)
    gathered = lax.all_to_all(spread, "dp", 0, 0).reshape(ranks * examples, rank_size * rank_size)
    folded = in_vmem(raw_kernel, jax.ShapeDtypeStruct((sections, 16, LANES), jnp.float32), "raw")(
        gathered, queries[0]
    )
    parts = lax.all_to_all(folded, "section", 0, 0)
    scores = in_vmem(
        functools.partial(scores_kernel, count=sections * rank_size * rank_size),
        jax.ShapeDtypeStruct((ranks * examples, share), jnp.float32),
        "scores",
    )(parts)
    return (scores, in_grad[None])


def solution(mesh):
    in_specs = (
        P("section", "dp", None),
        P("section", "dp", None),
        P("section", None),
        P("dp", None),
        P("dp"),
        P("section", None, None),
        P("section", None, None),
        P("section", "dp", None),
    )
    out_specs = (P(None, "dp"), P("section", "dp", None))
    return jax.shard_map(shards, mesh=mesh, in_specs=in_specs, out_specs=out_specs, check_vma=False)
```

```python
import functools
import math

import jax
import jax.numpy as jnp
from jax import lax
from jax.experimental import pallas as pl
from jax.experimental.pallas import tpu as pltpu
from jax.sharding import PartitionSpec as P

EPS = 1e-05
LANES = 128
SUBLANES = 16


def chain_kernel(place_ref, recv_ref, top_ref, *refs):
    *near_refs, out_ref, gain_ref, grad_ref, kept_ref, inv_ref, out_sem = refs
    sections, blocks = recv_ref.shape[:2]
    side = len(near_refs)
    width = blocks * 2 * LANES
    step = 4
    chunks = blocks // step
    row, column = place_ref[0] // side, place_ref[0] % side

    def leaving(group):
        span = pl.ds(group * side, side)
        return pltpu.make_async_copy(grad_ref.at[span], out_ref.at[span], out_sem.at[group])

    for down in range(side):
        for across in range(side):
            s = (row + side - down) % side * side + (column + side - across) % side
            gain_ref[s] = near_refs[down][across]
    grad_ref[sections - 1] = top_ref[...]

    def gain_of(s, k):
        return jnp.stack(
            [
                jnp.concatenate(
                    [
                        jnp.broadcast_to(gain_ref[s, pl.ds(2 * i, 1), :], (8, LANES)),
                        jnp.broadcast_to(gain_ref[s, pl.ds(2 * i + 1, 1), :], (8, LANES)),
                    ],
                    axis=0,
                )
                for i in range(k * step, (k + 1) * step)
            ]
        )

    def span(k):
        return pl.ds(k * step, step)

    def mean(v):
        v = jnp.sum(v, axis=0)
        v = v[:8] + v[8:]
        v = jnp.sum(v, axis=-1, keepdims=True) / width
        return jnp.broadcast_to(jnp.concatenate([v, v], axis=0), (SUBLANES, LANES))

    zero = jnp.zeros((step, SUBLANES, LANES), jnp.float32)
    for s in range(sections - 1, 0, -1):
        square = zero
        for k in range(chunks):
            x = recv_ref[s, span(k)].astype(jnp.float32)
            square = square + x * x
        inv_ref[s] = lax.rsqrt(mean(square) + EPS)

    def enter(s, k, g, inner):
        weighted = g * gain_of(s, k)
        kept_ref[span(k)] = g + inv_ref[s][None] * weighted
        return inner + weighted * recv_ref[s, span(k)].astype(jnp.float32)

    inner = zero
    for k in range(chunks):
        inner = enter(sections - 1, k, grad_ref[sections - 1, span(k)].astype(jnp.float32), inner)
    for s in range(sections - 1, 0, -1):
        inv = inv_ref[s]
        pull = (inv * inv * inv * mean(inner))[None]
        inner = zero
        for k in range(chunks):
            new = kept_ref[span(k)] - recv_ref[s, span(k)].astype(jnp.float32) * pull
            new = new.astype(jnp.bfloat16)
            grad_ref[s - 1, span(k)] = new
            if s > 1:
                inner = enter(s - 1, k, new.astype(jnp.float32), inner)
        if (s - 1) % side == 0:
            leaving((s - 1) // side).start()
    for group in range(side):
        leaving(group).wait()


def in_vmem(body, out_shape, name, scalars=0, scratch=()):
    def call(*args):
        specs = [pl.BlockSpec(memory_space=pltpu.SMEM)] * scalars
        specs += [pl.BlockSpec(memory_space=pltpu.VMEM)] * (len(args) - scalars)
        return pl.pallas_call(
            body,
            out_shape=out_shape,
            in_specs=specs,
            out_specs=pl.BlockSpec(memory_space=pltpu.VMEM),
            scratch_shapes=list(scratch),
            compiler_params=pltpu.CompilerParams(vmem_limit_bytes=8 * 1024 * 1024),
            name=name,
        )(*args)

    return call


def chain_all(place, recv, top, near):
    sections, blocks = recv.shape[:2]
    shape = (sections, blocks, SUBLANES, LANES)
    side = len(near)
    return pl.pallas_call(
        chain_kernel,
        out_shape=pltpu.HBM(shape, jnp.bfloat16),
        in_specs=[pl.BlockSpec(memory_space=pltpu.SMEM)] + [pl.BlockSpec(memory_space=pltpu.VMEM)] * (2 + side),
        out_specs=pl.BlockSpec(memory_space=pltpu.HBM),
        scratch_shapes=[
            pltpu.VMEM((sections, 2 * blocks, LANES), jnp.float32),
            pltpu.VMEM(shape, jnp.bfloat16),
            pltpu.VMEM(shape[1:], jnp.float32),
            pltpu.VMEM((sections, SUBLANES, LANES), jnp.float32),
            pltpu.SemaphoreType.DMA((side,)),
        ],
        compiler_params=pltpu.CompilerParams(vmem_limit_bytes=16 * 1024 * 1024),
        name="chain_all",
    )(place, recv, top, *near)


def front_kernel(held_ref, weight_ref, side_in_ref, out_ref):
    side_out = lax.dot_general(
        held_ref[...], weight_ref[...], (((1,), (1,)), ((), ())), preferred_element_type=jnp.float32
    ).astype(jnp.bfloat16)
    examples = out_ref.shape[0]
    rows = side_out.shape[0] // examples
    for e in range(examples):
        out_ref[e] = lax.dot_general(
            side_out[e * rows : (e + 1) * rows],
            side_in_ref[pl.ds(e * rows, rows), :],
            (((0,), (0,)), ((), ())),
            preferred_element_type=jnp.float32,
        ).astype(jnp.bfloat16)


def stage_kernel(queries_ref, out_ref, sem):
    copy = pltpu.make_async_copy(queries_ref, out_ref, sem)
    copy.start()
    copy.wait()


def staged(queries):
    return pl.pallas_call(
        stage_kernel,
        out_shape=pltpu.VMEM(queries.shape, queries.dtype),
        in_specs=[pl.BlockSpec(memory_space=pl.ANY)],
        out_specs=pl.BlockSpec(memory_space=pltpu.VMEM),
        scratch_shapes=[pltpu.SemaphoreType.DMA],
        compiler_params=pltpu.CompilerParams(vmem_limit_bytes=8 * 1024 * 1024),
        name="stage",
    )(queries)


def raw_kernel(place_ref, grads_ref, queries_ref, out_ref):
    chips, _, lanes = out_ref.shape
    share = queries_ref.shape[0] // chips
    grads = grads_ref[...]
    raw = lax.dot_general(
        grads, queries_ref[...], (((1,), (1,)), ((), ())), preferred_element_type=jnp.float32
    )
    wide = grads.astype(jnp.float32)
    squares = jnp.sum(wide * wide, axis=1, keepdims=True)
    fill = jnp.broadcast_to(squares, (grads.shape[0], lanes - share))
    for slot in range(chips):
        origin = (place_ref[0] + chips - slot) % chips
        out_ref[origin] = jnp.concatenate([raw[:, slot * share : (slot + 1) * share], fill], axis=1)


def fold_kernel(parts_ref, out_ref, *, share):
    chips, per = parts_ref.shape[:2]
    each = 8 // per
    raws, squares = [], []
    for j in range(chips // each):
        rows = jnp.concatenate([parts_ref[j * each + k] for k in range(each)], axis=0)
        raws.append(rows[:, :share])
        squares.append(rows[:, share : 2 * share])
    block = jnp.concatenate([jnp.concatenate(raws, axis=1), jnp.concatenate(squares, axis=1)], axis=0)
    for s in range(out_ref.shape[0]):
        out_ref[s] = block


def scores_kernel(parts_ref, out_ref, *, count):
    total = parts_ref[0]
    for s in range(1, parts_ref.shape[0]):
        total = total + parts_ref[s]
    scores = total[:8] / jnp.sqrt(total[8:] / count + 1e-06)
    share = out_ref.shape[1]
    for j in range(out_ref.shape[0] // 8):
        out_ref[pl.ds(8 * j, 8), :] = scores[:, j * share : (j + 1) * share]


def to_tiles(rows):
    count, width = rows.shape
    tiles = rows.reshape(count // 8, 8, width // LANES, LANES).transpose(0, 2, 1, 3)
    return tiles.reshape(count // 8, width // (2 * LANES), SUBLANES, LANES)


def from_tiles(tiles):
    groups, blocks = tiles.shape[:2]
    rows = tiles.reshape(groups, blocks * 2, 8, LANES).transpose(0, 2, 1, 3)
    return rows.reshape(groups * 8, blocks * 2 * LANES)


def chain_back(grad_rows, resid_rows, norm_gain):
    grad_f32 = grad_rows.astype(jnp.float32)
    resid_f32 = resid_rows.astype(jnp.float32)
    inv_rms = lax.rsqrt(jnp.mean(resid_f32 * resid_f32, axis=-1, keepdims=True) + EPS)
    weighted = grad_f32 * norm_gain
    inner_mean = jnp.mean(weighted * resid_f32, axis=-1, keepdims=True)
    result = grad_f32 + inv_rms * weighted - resid_f32 * (inv_rms * inv_rms * inv_rms) * inner_mean
    return result.astype(jnp.bfloat16)


def shards(hidden_acts, resid_stream, norm_scale, out_grad, lengths, proj_in, proj_out, queries):
    tok_rows, features = out_grad.shape
    examples = lengths.shape[0]
    seq_len = tok_rows // examples
    rank_size = proj_in.shape[1]
    sections = lax.axis_size("section")
    ranks = lax.axis_size("dp")
    share = queries.shape[1]
    me = lax.axis_index("section")
    resid_rows = resid_stream[0]
    norm_gain = norm_scale[0]

    side = math.isqrt(sections)
    grid = [(row, column) for row in range(side) for column in range(side)]

    def moved(value, down, across):
        pairs = [
            (row * side + column, (row + down) % side * side + (column + across) % side) for row, column in grid
        ]
        return lax.ppermute(value, "section", pairs)

    gain_tiles = norm_gain.reshape(-1, LANES)
    across = [moved(gain_tiles, 0, k) for k in range(1, side)]
    resid_first, across[0] = lax.optimization_barrier((resid_rows, across[0]))
    near = [jnp.stack([gain_tiles] + across)]
    near[0], own_queries = lax.optimization_barrier((near[0], queries[0]))
    near += [moved(near[0], k, 0) for k in range(1, side)]

    side_in = jnp.einsum(
        "tf,rf->tr", hidden_acts[0], proj_in[0], preferred_element_type=jnp.float32
    ).astype(jnp.bfloat16)

    chips = ranks // 2

    def around(value, steps):
        return lax.ppermute(value, "dp", [(i, (i + 2 * steps) % ranks) for i in range(ranks)])

    def longer(ring, steps, count):
        for _ in range(count):
            ring.append(around(ring[-1], steps))

    up, down = [own_queries], [own_queries]
    longer(up, 1, 1)
    longer(down, -1, 1)

    own = tok_rows // sections
    recv = lax.all_to_all(to_tiles(resid_first), "section", 0, 0)
    recv, side_in, up, down = lax.optimization_barrier((recv, side_in, up, down))
    longer(up, 1, chips // 2 - 1)
    longer(down, -1, chips - 2 - chips // 2)
    all_queries = jnp.concatenate(up + down[:0:-1])
    own_rows = lax.dynamic_slice_in_dim(out_grad, me * own, own, axis=0)
    own_slots = me * own + jnp.arange(own, dtype=jnp.int32)
    own_live = own_slots % seq_len < jnp.take(lengths, own_slots // seq_len)
    own_top = jnp.where(own_live[:, None], own_rows, jnp.zeros_like(own_rows))
    grads = chain_all(me.astype(jnp.int32).reshape(1), recv, to_tiles(own_top)[0], near)
    held, all_queries = lax.optimization_barrier((lax.all_to_all(grads, "section", 0, 0), all_queries))
    held_grad = from_tiles(held)

    outer = in_vmem(front_kernel, jax.ShapeDtypeStruct((examples, rank_size, rank_size), jnp.bfloat16), "front")(
        held_grad, proj_out[0], side_in
    )
    example_grads = outer.reshape(examples, rank_size * rank_size)
    example_grads, all_queries = lax.optimization_barrier((example_grads, all_queries))
    all_queries = staged(all_queries)
    rank = lax.axis_index("dp")
    other_grads = lax.ppermute(example_grads, "dp", [(i, i ^ 1) for i in range(ranks)])
    first, second = (jnp.where(rank % 2 == k, example_grads, other_grads) for k in range(2))
    raw = in_vmem(
        raw_kernel,
        jax.ShapeDtypeStruct((chips, 2 * examples, LANES), jnp.float32),
        "raw",
        scalars=1,
    )((rank // 2).astype(jnp.int32).reshape(1), jnp.concatenate([first, second]), all_queries)
    held_grad, raw = lax.optimization_barrier((held_grad, raw))
    in_grad = chain_back(held_grad, resid_rows, norm_gain)
    same_core = [list(range(core, ranks, 2)) for core in range(2)]
    raw = lax.all_to_all(raw, "dp", 0, 0, axis_index_groups=same_core)
    folded = in_vmem(
        functools.partial(fold_kernel, share=queries.shape[1]),
        jax.ShapeDtypeStruct((sections, 16, LANES), jnp.float32),
        "fold",
    )(raw)
    parts = lax.all_to_all(folded, "section", 0, 0)
    scores = in_vmem(
        functools.partial(scores_kernel, count=sections * rank_size * rank_size),
        jax.ShapeDtypeStruct((ranks * examples, share), jnp.float32),
        "scores",
    )(parts)
    return (scores, in_grad[None])


def solution(mesh):
    in_specs = (
        P("section", "dp", None),
        P("section", "dp", None),
        P("section", None),
        P("dp", None),
        P("dp"),
        P("section", None, None),
        P("section", None, None),
        P("section", "dp", None),
    )
    out_specs = (P(None, "dp"), P("section", "dp", None))
    return jax.shard_map(shards, mesh=mesh, in_specs=in_specs, out_specs=out_specs, check_vma=False)
```

```python
import functools
import math

import jax
import jax.numpy as jnp
from jax import lax
from jax.experimental import pallas as pl
from jax.experimental.pallas import tpu as pltpu
from jax.sharding import PartitionSpec as P

EPS = 1e-05
LANES = 128
SUBLANES = 16


def chain_kernel(place_ref, recv_ref, top_ref, *refs):
    *near_refs, out_ref, gain_ref, grad_ref, kept_ref, inv_ref, out_sem = refs
    sections, blocks = recv_ref.shape[:2]
    side = len(near_refs)
    width = blocks * 2 * LANES
    step = 4
    chunks = blocks // step
    row, column = place_ref[0] // side, place_ref[0] % side

    def leaving(group):
        span = pl.ds(group * side, side)
        return pltpu.make_async_copy(grad_ref.at[span], out_ref.at[span], out_sem.at[group])

    for down in range(side):
        for across in range(side):
            s = (row + side - down) % side * side + (column + side - across) % side
            gain_ref[s] = near_refs[down][across]
    grad_ref[sections - 1] = top_ref[...]

    def gain_of(s, k):
        return jnp.stack(
            [
                jnp.concatenate(
                    [
                        jnp.broadcast_to(gain_ref[s, pl.ds(2 * i, 1), :], (8, LANES)),
                        jnp.broadcast_to(gain_ref[s, pl.ds(2 * i + 1, 1), :], (8, LANES)),
                    ],
                    axis=0,
                )
                for i in range(k * step, (k + 1) * step)
            ]
        )

    def span(k):
        return pl.ds(k * step, step)

    def mean(v):
        v = jnp.sum(v, axis=0)
        v = v[:8] + v[8:]
        v = jnp.sum(v, axis=-1, keepdims=True) / width
        return jnp.broadcast_to(jnp.concatenate([v, v], axis=0), (SUBLANES, LANES))

    zero = jnp.zeros((step, SUBLANES, LANES), jnp.float32)
    for s in range(sections - 1, 0, -1):
        square = zero
        for k in range(chunks):
            x = recv_ref[s, span(k)].astype(jnp.float32)
            square = square + x * x
        inv_ref[s] = lax.rsqrt(mean(square) + EPS)

    def enter(s, k, g, inner):
        weighted = g * gain_of(s, k)
        kept_ref[span(k)] = g + inv_ref[s][None] * weighted
        return inner + weighted * recv_ref[s, span(k)].astype(jnp.float32)

    inner = zero
    for k in range(chunks):
        inner = enter(sections - 1, k, grad_ref[sections - 1, span(k)].astype(jnp.float32), inner)
    for s in range(sections - 1, 0, -1):
        inv = inv_ref[s]
        pull = (inv * inv * inv * mean(inner))[None]
        inner = zero
        for k in range(chunks):
            new = kept_ref[span(k)] - recv_ref[s, span(k)].astype(jnp.float32) * pull
            new = new.astype(jnp.bfloat16)
            grad_ref[s - 1, span(k)] = new
            if s > 1:
                inner = enter(s - 1, k, new.astype(jnp.float32), inner)
        if (s - 1) % side == 0:
            leaving((s - 1) // side).start()
    for group in range(side):
        leaving(group).wait()


def in_vmem(body, out_shape, name, scalars=0, scratch=()):
    def call(*args):
        specs = [pl.BlockSpec(memory_space=pltpu.SMEM)] * scalars
        specs += [pl.BlockSpec(memory_space=pltpu.VMEM)] * (len(args) - scalars)
        return pl.pallas_call(
            body,
            out_shape=out_shape,
            in_specs=specs,
            out_specs=pl.BlockSpec(memory_space=pltpu.VMEM),
            scratch_shapes=list(scratch),
            compiler_params=pltpu.CompilerParams(vmem_limit_bytes=8 * 1024 * 1024),
            name=name,
        )(*args)

    return call


def chain_all(place, recv, top, near):
    sections, blocks = recv.shape[:2]
    shape = (sections, blocks, SUBLANES, LANES)
    side = len(near)
    return pl.pallas_call(
        chain_kernel,
        out_shape=pltpu.HBM(shape, jnp.bfloat16),
        in_specs=[pl.BlockSpec(memory_space=pltpu.SMEM)] + [pl.BlockSpec(memory_space=pltpu.VMEM)] * (2 + side),
        out_specs=pl.BlockSpec(memory_space=pltpu.HBM),
        scratch_shapes=[
            pltpu.VMEM((sections, 2 * blocks, LANES), jnp.float32),
            pltpu.VMEM(shape, jnp.bfloat16),
            pltpu.VMEM(shape[1:], jnp.float32),
            pltpu.VMEM((sections, SUBLANES, LANES), jnp.float32),
            pltpu.SemaphoreType.DMA((side,)),
        ],
        compiler_params=pltpu.CompilerParams(vmem_limit_bytes=16 * 1024 * 1024),
        name="chain_all",
    )(place, recv, top, *near)


def front_kernel(held_ref, weight_ref, side_in_ref, out_ref):
    side_out = lax.dot_general(
        held_ref[...], weight_ref[...], (((1,), (1,)), ((), ())), preferred_element_type=jnp.float32
    ).astype(jnp.bfloat16)
    examples = out_ref.shape[0]
    rows = side_out.shape[0] // examples
    for e in range(examples):
        out_ref[e] = lax.dot_general(
            side_out[e * rows : (e + 1) * rows],
            side_in_ref[pl.ds(e * rows, rows), :],
            (((0,), (0,)), ((), ())),
            preferred_element_type=jnp.float32,
        ).astype(jnp.bfloat16)


def stage_kernel(queries_ref, out_ref, sem):
    copy = pltpu.make_async_copy(queries_ref, out_ref, sem)
    copy.start()
    copy.wait()


def staged(queries):
    return pl.pallas_call(
        stage_kernel,
        out_shape=pltpu.VMEM(queries.shape, queries.dtype),
        in_specs=[pl.BlockSpec(memory_space=pl.ANY)],
        out_specs=pl.BlockSpec(memory_space=pltpu.VMEM),
        scratch_shapes=[pltpu.SemaphoreType.DMA],
        compiler_params=pltpu.CompilerParams(vmem_limit_bytes=8 * 1024 * 1024),
        name="stage",
    )(queries)


def raw_kernel(place_ref, grads_ref, queries_ref, out_ref):
    chips, _, lanes = out_ref.shape
    share = queries_ref.shape[0] // chips
    grads = grads_ref[...]
    raw = lax.dot_general(
        grads, queries_ref[...], (((1,), (1,)), ((), ())), preferred_element_type=jnp.float32
    )
    wide = grads.astype(jnp.float32)
    squares = jnp.sum(wide * wide, axis=1, keepdims=True)
    fill = jnp.broadcast_to(squares, (grads.shape[0], lanes - share))
    for slot in range(chips):
        origin = (place_ref[0] + chips - slot) % chips
        out_ref[origin] = jnp.concatenate([raw[:, slot * share : (slot + 1) * share], fill], axis=1)


def fold_kernel(parts_ref, out_ref, *, share):
    chips, per = parts_ref.shape[:2]
    each = 8 // per
    raws, squares = [], []
    for j in range(chips // each):
        rows = jnp.concatenate([parts_ref[j * each + k] for k in range(each)], axis=0)
        raws.append(rows[:, :share])
        squares.append(rows[:, share : 2 * share])
    block = jnp.concatenate([jnp.concatenate(raws, axis=1), jnp.concatenate(squares, axis=1)], axis=0)
    for s in range(out_ref.shape[0]):
        out_ref[s] = block


def scores_kernel(parts_ref, out_ref, *, count):
    total = parts_ref[0]
    for s in range(1, parts_ref.shape[0]):
        total = total + parts_ref[s]
    scores = total[:8] / jnp.sqrt(total[8:] / count + 1e-06)
    share = out_ref.shape[1]
    for j in range(out_ref.shape[0] // 8):
        out_ref[pl.ds(8 * j, 8), :] = scores[:, j * share : (j + 1) * share]


def to_tiles(rows):
    count, width = rows.shape
    tiles = rows.reshape(count // 8, 8, width // LANES, LANES).transpose(0, 2, 1, 3)
    return tiles.reshape(count // 8, width // (2 * LANES), SUBLANES, LANES)


def from_tiles(tiles):
    groups, blocks = tiles.shape[:2]
    rows = tiles.reshape(groups, blocks * 2, 8, LANES).transpose(0, 2, 1, 3)
    return rows.reshape(groups * 8, blocks * 2 * LANES)


def chain_back(grad_rows, resid_rows, norm_gain):
    grad_f32 = grad_rows.astype(jnp.float32)
    resid_f32 = resid_rows.astype(jnp.float32)
    inv_rms = lax.rsqrt(jnp.mean(resid_f32 * resid_f32, axis=-1, keepdims=True) + EPS)
    weighted = grad_f32 * norm_gain
    inner_mean = jnp.mean(weighted * resid_f32, axis=-1, keepdims=True)
    result = grad_f32 + inv_rms * weighted - resid_f32 * (inv_rms * inv_rms * inv_rms) * inner_mean
    return result.astype(jnp.bfloat16)


def shards(hidden_acts, resid_stream, norm_scale, out_grad, lengths, proj_in, proj_out, queries):
    tok_rows, features = out_grad.shape
    examples = lengths.shape[0]
    seq_len = tok_rows // examples
    rank_size = proj_in.shape[1]
    sections = lax.axis_size("section")
    ranks = lax.axis_size("dp")
    share = queries.shape[1]
    me = lax.axis_index("section")
    resid_rows = resid_stream[0]
    norm_gain = norm_scale[0]

    side = math.isqrt(sections)
    grid = [(row, column) for row in range(side) for column in range(side)]

    def moved(value, down, across):
        pairs = [
            (row * side + column, (row + down) % side * side + (column + across) % side) for row, column in grid
        ]
        return lax.ppermute(value, "section", pairs)

    gain_tiles = norm_gain.reshape(-1, LANES)
    across = [moved(gain_tiles, 0, k) for k in range(1, side)]
    resid_first = resid_rows
    near = [jnp.stack([gain_tiles] + across)]
    near[0], own_queries = lax.optimization_barrier((near[0], queries[0]))
    near += [moved(near[0], k, 0) for k in range(1, side)]

    side_in = jnp.einsum(
        "tf,rf->tr", hidden_acts[0], proj_in[0], preferred_element_type=jnp.float32
    ).astype(jnp.bfloat16)

    chips = ranks // 2

    def around(value, steps):
        return lax.ppermute(value, "dp", [(i, (i + 2 * steps) % ranks) for i in range(ranks)])

    def longer(ring, steps, count):
        for _ in range(count):
            ring.append(around(ring[-1], steps))

    up, down = [own_queries], [own_queries]
    longer(up, 1, 1)
    longer(down, -1, 1)

    own = tok_rows // sections
    recv = lax.all_to_all(to_tiles(resid_first), "section", 0, 0)
    recv, side_in, up, down = lax.optimization_barrier((recv, side_in, up, down))
    longer(up, 1, chips // 2 - 1)
    longer(down, -1, chips - 2 - chips // 2)
    all_queries = jnp.concatenate(up + down[:0:-1])
    own_rows = lax.dynamic_slice_in_dim(out_grad, me * own, own, axis=0)
    own_slots = me * own + jnp.arange(own, dtype=jnp.int32)
    own_live = own_slots % seq_len < jnp.take(lengths, own_slots // seq_len)
    own_top = jnp.where(own_live[:, None], own_rows, jnp.zeros_like(own_rows))
    grads = chain_all(me.astype(jnp.int32).reshape(1), recv, to_tiles(own_top)[0], near)
    held, all_queries = lax.optimization_barrier((lax.all_to_all(grads, "section", 0, 0), all_queries))
    held_grad = from_tiles(held)

    outer = in_vmem(front_kernel, jax.ShapeDtypeStruct((examples, rank_size, rank_size), jnp.bfloat16), "front")(
        held_grad, proj_out[0], side_in
    )
    example_grads = outer.reshape(examples, rank_size * rank_size)
    example_grads, all_queries = lax.optimization_barrier((example_grads, all_queries))
    all_queries = staged(all_queries)
    rank = lax.axis_index("dp")
    other_grads = lax.ppermute(example_grads, "dp", [(i, i ^ 1) for i in range(ranks)])
    first, second = (jnp.where(rank % 2 == k, example_grads, other_grads) for k in range(2))
    raw = in_vmem(
        raw_kernel,
        jax.ShapeDtypeStruct((chips, 2 * examples, LANES), jnp.float32),
        "raw",
        scalars=1,
    )((rank // 2).astype(jnp.int32).reshape(1), jnp.concatenate([first, second]), all_queries)
    held_grad, raw = lax.optimization_barrier((held_grad, raw))
    in_grad = chain_back(held_grad, resid_rows, norm_gain)
    same_core = [list(range(core, ranks, 2)) for core in range(2)]
    raw = lax.all_to_all(raw, "dp", 0, 0, axis_index_groups=same_core)
    folded = in_vmem(
        functools.partial(fold_kernel, share=queries.shape[1]),
        jax.ShapeDtypeStruct((sections, 16, LANES), jnp.float32),
        "fold",
    )(raw)
    parts = lax.all_to_all(folded, "section", 0, 0)
    scores = in_vmem(
        functools.partial(scores_kernel, count=sections * rank_size * rank_size),
        jax.ShapeDtypeStruct((ranks * examples, share), jnp.float32),
        "scores",
    )(parts)
    return (scores, in_grad[None])


def solution(mesh):
    in_specs = (
        P("section", "dp", None),
        P("section", "dp", None),
        P("section", None),
        P("dp", None),
        P("dp"),
        P("section", None, None),
        P("section", None, None),
        P("section", "dp", None),
    )
    out_specs = (P(None, "dp"), P("section", "dp", None))
    return jax.shard_map(shards, mesh=mesh, in_specs=in_specs, out_specs=out_specs, check_vma=False)
```

```python
import functools
import math

import jax
import jax.numpy as jnp
from jax import lax
from jax.experimental import pallas as pl
from jax.experimental.pallas import tpu as pltpu
from jax.sharding import PartitionSpec as P

EPS = 1e-05
LANES = 128
SUBLANES = 16


def chain_kernel(place_ref, recv_ref, top_ref, *refs):
    *near_refs, out_ref, gain_ref, grad_ref, kept_ref, inv_ref, out_sem = refs
    sections, blocks = recv_ref.shape[:2]
    side = len(near_refs)
    width = blocks * 2 * LANES
    step = 4
    chunks = blocks // step
    row, column = place_ref[0] // side, place_ref[0] % side

    cuts = [0, 1, 2] + list(range(side, sections + 1, side))

    def leaving(group):
        span = pl.ds(cuts[group], cuts[group + 1] - cuts[group])
        return pltpu.make_async_copy(grad_ref.at[span], out_ref.at[span], out_sem.at[group])

    for down in range(side):
        for across in range(side):
            s = (row + side - down) % side * side + (column + side - across) % side
            gain_ref[s] = near_refs[down][across]
    grad_ref[sections - 1] = top_ref[...]

    def gain_of(s, k):
        return jnp.stack(
            [
                jnp.concatenate(
                    [
                        jnp.broadcast_to(gain_ref[s, pl.ds(2 * i, 1), :], (8, LANES)),
                        jnp.broadcast_to(gain_ref[s, pl.ds(2 * i + 1, 1), :], (8, LANES)),
                    ],
                    axis=0,
                )
                for i in range(k * step, (k + 1) * step)
            ]
        )

    def span(k):
        return pl.ds(k * step, step)

    def mean(v):
        v = jnp.sum(v, axis=0)
        v = v[:8] + v[8:]
        v = jnp.sum(v, axis=-1, keepdims=True) / width
        return jnp.broadcast_to(jnp.concatenate([v, v], axis=0), (SUBLANES, LANES))

    zero = jnp.zeros((step, SUBLANES, LANES), jnp.float32)
    for s in range(sections - 1, 0, -1):
        square = zero
        for k in range(chunks):
            x = recv_ref[s, span(k)].astype(jnp.float32)
            square = square + x * x
        inv_ref[s] = lax.rsqrt(mean(square) + EPS)

    def enter(s, k, g, inner):
        weighted = g * gain_of(s, k)
        kept_ref[span(k)] = g + inv_ref[s][None] * weighted
        return inner + weighted * recv_ref[s, span(k)].astype(jnp.float32)

    inner = zero
    for k in range(chunks):
        inner = enter(sections - 1, k, grad_ref[sections - 1, span(k)].astype(jnp.float32), inner)
    for s in range(sections - 1, 0, -1):
        inv = inv_ref[s]
        pull = (inv * inv * inv * mean(inner))[None]
        inner = zero
        for k in range(chunks):
            new = kept_ref[span(k)] - recv_ref[s, span(k)].astype(jnp.float32) * pull
            new = new.astype(jnp.bfloat16)
            grad_ref[s - 1, span(k)] = new
            if s > 1:
                inner = enter(s - 1, k, new.astype(jnp.float32), inner)
        if s - 1 in cuts:
            leaving(cuts.index(s - 1)).start()
    for group in range(len(cuts) - 1):
        leaving(group).wait()


def in_vmem(body, out_shape, name, scalars=0, scratch=()):
    def call(*args):
        specs = [pl.BlockSpec(memory_space=pltpu.SMEM)] * scalars
        specs += [pl.BlockSpec(memory_space=pltpu.VMEM)] * (len(args) - scalars)
        return pl.pallas_call(
            body,
            out_shape=out_shape,
            in_specs=specs,
            out_specs=pl.BlockSpec(memory_space=pltpu.VMEM),
            scratch_shapes=list(scratch),
            compiler_params=pltpu.CompilerParams(vmem_limit_bytes=8 * 1024 * 1024),
            name=name,
        )(*args)

    return call


def chain_all(place, recv, top, near):
    sections, blocks = recv.shape[:2]
    shape = (sections, blocks, SUBLANES, LANES)
    side = len(near)
    return pl.pallas_call(
        chain_kernel,
        out_shape=pltpu.HBM(shape, jnp.bfloat16),
        in_specs=[pl.BlockSpec(memory_space=pltpu.SMEM)] + [pl.BlockSpec(memory_space=pltpu.VMEM)] * (2 + side),
        out_specs=pl.BlockSpec(memory_space=pltpu.HBM),
        scratch_shapes=[
            pltpu.VMEM((sections, 2 * blocks, LANES), jnp.float32),
            pltpu.VMEM(shape, jnp.bfloat16),
            pltpu.VMEM(shape[1:], jnp.float32),
            pltpu.VMEM((sections, SUBLANES, LANES), jnp.float32),
            pltpu.SemaphoreType.DMA((side + 2,)),
        ],
        compiler_params=pltpu.CompilerParams(vmem_limit_bytes=16 * 1024 * 1024),
        name="chain_all",
    )(place, recv, top, *near)


def front_kernel(held_ref, weight_ref, side_in_ref, out_ref):
    side_out = lax.dot_general(
        held_ref[...], weight_ref[...], (((1,), (1,)), ((), ())), preferred_element_type=jnp.float32
    ).astype(jnp.bfloat16)
    examples = out_ref.shape[0]
    rows = side_out.shape[0] // examples
    for e in range(examples):
        out_ref[e] = lax.dot_general(
            side_out[e * rows : (e + 1) * rows],
            side_in_ref[pl.ds(e * rows, rows), :],
            (((0,), (0,)), ((), ())),
            preferred_element_type=jnp.float32,
        ).astype(jnp.bfloat16)


def stage_kernel(queries_ref, out_ref, sem):
    copy = pltpu.make_async_copy(queries_ref, out_ref, sem)
    copy.start()
    copy.wait()


def staged(queries):
    return pl.pallas_call(
        stage_kernel,
        out_shape=pltpu.VMEM(queries.shape, queries.dtype),
        in_specs=[pl.BlockSpec(memory_space=pl.ANY)],
        out_specs=pl.BlockSpec(memory_space=pltpu.VMEM),
        scratch_shapes=[pltpu.SemaphoreType.DMA],
        compiler_params=pltpu.CompilerParams(vmem_limit_bytes=8 * 1024 * 1024),
        name="stage",
    )(queries)


def raw_kernel(place_ref, grads_ref, queries_ref, out_ref):
    chips, _, lanes = out_ref.shape
    share = queries_ref.shape[0] // chips
    grads = grads_ref[...]
    raw = lax.dot_general(
        grads, queries_ref[...], (((1,), (1,)), ((), ())), preferred_element_type=jnp.float32
    )
    wide = grads.astype(jnp.float32)
    squares = jnp.sum(wide * wide, axis=1, keepdims=True)
    fill = jnp.broadcast_to(squares, (grads.shape[0], lanes - share))
    for slot in range(chips):
        origin = (place_ref[0] + chips - slot) % chips
        out_ref[origin] = jnp.concatenate([raw[:, slot * share : (slot + 1) * share], fill], axis=1)


def fold_kernel(parts_ref, out_ref, *, share):
    chips, per = parts_ref.shape[:2]
    each = 8 // per
    raws, squares = [], []
    for j in range(chips // each):
        rows = jnp.concatenate([parts_ref[j * each + k] for k in range(each)], axis=0)
        raws.append(rows[:, :share])
        squares.append(rows[:, share : 2 * share])
    block = jnp.concatenate([jnp.concatenate(raws, axis=1), jnp.concatenate(squares, axis=1)], axis=0)
    for s in range(out_ref.shape[0]):
        out_ref[s] = block


def scores_kernel(parts_ref, out_ref, *, count):
    total = parts_ref[0]
    for s in range(1, parts_ref.shape[0]):
        total = total + parts_ref[s]
    scores = total[:8] / jnp.sqrt(total[8:] / count + 1e-06)
    share = out_ref.shape[1]
    for j in range(out_ref.shape[0] // 8):
        out_ref[pl.ds(8 * j, 8), :] = scores[:, j * share : (j + 1) * share]


def to_tiles(rows):
    count, width = rows.shape
    tiles = rows.reshape(count // 8, 8, width // LANES, LANES).transpose(0, 2, 1, 3)
    return tiles.reshape(count // 8, width // (2 * LANES), SUBLANES, LANES)


def from_tiles(tiles):
    groups, blocks = tiles.shape[:2]
    rows = tiles.reshape(groups, blocks * 2, 8, LANES).transpose(0, 2, 1, 3)
    return rows.reshape(groups * 8, blocks * 2 * LANES)


def chain_back(grad_rows, resid_rows, norm_gain):
    grad_f32 = grad_rows.astype(jnp.float32)
    resid_f32 = resid_rows.astype(jnp.float32)
    inv_rms = lax.rsqrt(jnp.mean(resid_f32 * resid_f32, axis=-1, keepdims=True) + EPS)
    weighted = grad_f32 * norm_gain
    inner_mean = jnp.mean(weighted * resid_f32, axis=-1, keepdims=True)
    result = grad_f32 + inv_rms * weighted - resid_f32 * (inv_rms * inv_rms * inv_rms) * inner_mean
    return result.astype(jnp.bfloat16)


def shards(hidden_acts, resid_stream, norm_scale, out_grad, lengths, proj_in, proj_out, queries):
    tok_rows, features = out_grad.shape
    examples = lengths.shape[0]
    seq_len = tok_rows // examples
    rank_size = proj_in.shape[1]
    sections = lax.axis_size("section")
    ranks = lax.axis_size("dp")
    share = queries.shape[1]
    me = lax.axis_index("section")
    resid_rows = resid_stream[0]
    norm_gain = norm_scale[0]

    side = math.isqrt(sections)
    grid = [(row, column) for row in range(side) for column in range(side)]

    def moved(value, down, across):
        pairs = [
            (row * side + column, (row + down) % side * side + (column + across) % side) for row, column in grid
        ]
        return lax.ppermute(value, "section", pairs)

    gain_tiles = norm_gain.reshape(-1, LANES)
    across = [moved(gain_tiles, 0, k) for k in range(1, side)]
    resid_first = resid_rows
    near = [jnp.stack([gain_tiles] + across)]
    near[0], own_queries = lax.optimization_barrier((near[0], queries[0]))
    near += [moved(near[0], k, 0) for k in range(1, side)]

    side_in = jnp.einsum(
        "tf,rf->tr", hidden_acts[0], proj_in[0], preferred_element_type=jnp.float32
    ).astype(jnp.bfloat16)

    chips = ranks // 2

    def around(value, steps):
        return lax.ppermute(value, "dp", [(i, (i + 2 * steps) % ranks) for i in range(ranks)])

    def longer(ring, steps, count):
        for _ in range(count):
            ring.append(around(ring[-1], steps))

    up, down = [own_queries], [own_queries]
    longer(up, 1, 1)
    longer(down, -1, 1)

    own = tok_rows // sections
    recv = lax.all_to_all(to_tiles(resid_first), "section", 0, 0)
    recv, side_in, up, down = lax.optimization_barrier((recv, side_in, up, down))
    longer(up, 1, chips // 2 - 1)
    longer(down, -1, chips - 2 - chips // 2)
    all_queries = jnp.concatenate(up + down[:0:-1])
    own_rows = lax.dynamic_slice_in_dim(out_grad, me * own, own, axis=0)
    own_slots = me * own + jnp.arange(own, dtype=jnp.int32)
    own_live = own_slots % seq_len < jnp.take(lengths, own_slots // seq_len)
    own_top = jnp.where(own_live[:, None], own_rows, jnp.zeros_like(own_rows))
    grads = chain_all(me.astype(jnp.int32).reshape(1), recv, to_tiles(own_top)[0], near)
    held, all_queries = lax.optimization_barrier((lax.all_to_all(grads, "section", 0, 0), all_queries))
    held_grad = from_tiles(held)

    outer = in_vmem(front_kernel, jax.ShapeDtypeStruct((examples, rank_size, rank_size), jnp.bfloat16), "front")(
        held_grad, proj_out[0], side_in
    )
    example_grads = outer.reshape(examples, rank_size * rank_size)
    example_grads, all_queries = lax.optimization_barrier((example_grads, all_queries))
    all_queries = staged(all_queries)
    rank = lax.axis_index("dp")
    other_grads = lax.ppermute(example_grads, "dp", [(i, i ^ 1) for i in range(ranks)])
    first, second = (jnp.where(rank % 2 == k, example_grads, other_grads) for k in range(2))
    raw = in_vmem(
        raw_kernel,
        jax.ShapeDtypeStruct((chips, 2 * examples, LANES), jnp.float32),
        "raw",
        scalars=1,
    )((rank // 2).astype(jnp.int32).reshape(1), jnp.concatenate([first, second]), all_queries)
    held_grad, raw = lax.optimization_barrier((held_grad, raw))
    in_grad = chain_back(held_grad, resid_rows, norm_gain)
    same_core = [list(range(core, ranks, 2)) for core in range(2)]
    raw = lax.all_to_all(raw, "dp", 0, 0, axis_index_groups=same_core)
    folded = in_vmem(
        functools.partial(fold_kernel, share=queries.shape[1]),
        jax.ShapeDtypeStruct((sections, 16, LANES), jnp.float32),
        "fold",
    )(raw)
    parts = lax.all_to_all(folded, "section", 0, 0)
    scores = in_vmem(
        functools.partial(scores_kernel, count=sections * rank_size * rank_size),
        jax.ShapeDtypeStruct((ranks * examples, share), jnp.float32),
        "scores",
    )(parts)
    return (scores, in_grad[None])


def solution(mesh):
    in_specs = (
        P("section", "dp", None),
        P("section", "dp", None),
        P("section", None),
        P("dp", None),
        P("dp"),
        P("section", None, None),
        P("section", None, None),
        P("section", "dp", None),
    )
    out_specs = (P(None, "dp"), P("section", "dp", None))
    return jax.shard_map(shards, mesh=mesh, in_specs=in_specs, out_specs=out_specs, check_vma=False)
```

```python
import functools
import math

import jax
import jax.numpy as jnp
from jax import lax
from jax.experimental import pallas as pl
from jax.experimental.pallas import tpu as pltpu
from jax.sharding import PartitionSpec as P

EPS = 1e-05
LANES = 128
SUBLANES = 16


def chain_kernel(place_ref, recv_ref, top_ref, *refs):
    *near_refs, out_ref, gain_ref, grad_ref, kept_ref, inv_ref, out_sem = refs
    sections, blocks = recv_ref.shape[:2]
    side = len(near_refs)
    width = blocks * 2 * LANES
    step = 4
    chunks = blocks // step
    row, column = place_ref[0] // side, place_ref[0] % side

    cuts = [0, 1, 2] + list(range(side, sections + 1, side))

    def leaving(group):
        span = pl.ds(cuts[group], cuts[group + 1] - cuts[group])
        return pltpu.make_async_copy(grad_ref.at[span], out_ref.at[span], out_sem.at[group])

    for down in range(side):
        for across in range(side):
            s = (row + side - down) % side * side + (column + side - across) % side
            gain_ref[s] = near_refs[down][across]
    grad_ref[sections - 1] = top_ref[...]

    def gain_of(s, k):
        return jnp.stack(
            [
                jnp.concatenate(
                    [
                        jnp.broadcast_to(gain_ref[s, pl.ds(2 * i, 1), :], (8, LANES)),
                        jnp.broadcast_to(gain_ref[s, pl.ds(2 * i + 1, 1), :], (8, LANES)),
                    ],
                    axis=0,
                )
                for i in range(k * step, (k + 1) * step)
            ]
        )

    def span(k):
        return pl.ds(k * step, step)

    def mean(v):
        v = jnp.sum(v, axis=0)
        v = v[:8] + v[8:]
        parts = []
        for _ in range(3):
            parts.append(v.astype(jnp.bfloat16))
            v = v - parts[-1].astype(jnp.float32)
        ones = jnp.ones((3 * LANES, LANES), jnp.bfloat16)
        v = jnp.dot(jnp.concatenate(parts, axis=1), ones, preferred_element_type=jnp.float32) / width
        return jnp.concatenate([v, v], axis=0)

    zero = jnp.zeros((step, SUBLANES, LANES), jnp.float32)
    for s in range(sections - 1, 0, -1):
        square = zero
        for k in range(chunks):
            x = recv_ref[s, span(k)].astype(jnp.float32)
            square = square + x * x
        inv_ref[s] = lax.rsqrt(mean(square) + EPS)

    def enter(s, k, g, inner):
        weighted = g * gain_of(s, k)
        kept_ref[span(k)] = g + inv_ref[s][None] * weighted
        return inner + weighted * recv_ref[s, span(k)].astype(jnp.float32)

    inner = zero
    for k in range(chunks):
        inner = enter(sections - 1, k, grad_ref[sections - 1, span(k)].astype(jnp.float32), inner)
    for s in range(sections - 1, 0, -1):
        inv = inv_ref[s]
        pull = (inv * inv * inv * mean(inner))[None]
        inner = zero
        for k in range(chunks):
            new = kept_ref[span(k)] - recv_ref[s, span(k)].astype(jnp.float32) * pull
            new = new.astype(jnp.bfloat16)
            grad_ref[s - 1, span(k)] = new
            if s > 1:
                inner = enter(s - 1, k, new.astype(jnp.float32), inner)
        if s - 1 in cuts:
            leaving(cuts.index(s - 1)).start()
    for group in range(len(cuts) - 1):
        leaving(group).wait()


def in_vmem(body, out_shape, name, scalars=0, scratch=()):
    def call(*args):
        specs = [pl.BlockSpec(memory_space=pltpu.SMEM)] * scalars
        specs += [pl.BlockSpec(memory_space=pltpu.VMEM)] * (len(args) - scalars)
        return pl.pallas_call(
            body,
            out_shape=out_shape,
            in_specs=specs,
            out_specs=pl.BlockSpec(memory_space=pltpu.VMEM),
            scratch_shapes=list(scratch),
            compiler_params=pltpu.CompilerParams(vmem_limit_bytes=8 * 1024 * 1024),
            name=name,
        )(*args)

    return call


def chain_all(place, recv, top, near):
    sections, blocks = recv.shape[:2]
    shape = (sections, blocks, SUBLANES, LANES)
    side = len(near)
    return pl.pallas_call(
        chain_kernel,
        out_shape=pltpu.HBM(shape, jnp.bfloat16),
        in_specs=[pl.BlockSpec(memory_space=pltpu.SMEM)] + [pl.BlockSpec(memory_space=pltpu.VMEM)] * (2 + side),
        out_specs=pl.BlockSpec(memory_space=pltpu.HBM),
        scratch_shapes=[
            pltpu.VMEM((sections, 2 * blocks, LANES), jnp.float32),
            pltpu.VMEM(shape, jnp.bfloat16),
            pltpu.VMEM(shape[1:], jnp.float32),
            pltpu.VMEM((sections, SUBLANES, LANES), jnp.float32),
            pltpu.SemaphoreType.DMA((side + 2,)),
        ],
        compiler_params=pltpu.CompilerParams(vmem_limit_bytes=16 * 1024 * 1024),
        name="chain_all",
    )(place, recv, top, *near)


def front_kernel(held_ref, weight_ref, side_in_ref, out_ref):
    side_out = lax.dot_general(
        held_ref[...], weight_ref[...], (((1,), (1,)), ((), ())), preferred_element_type=jnp.float32
    ).astype(jnp.bfloat16)
    examples = out_ref.shape[0]
    rows = side_out.shape[0] // examples
    for e in range(examples):
        out_ref[e] = lax.dot_general(
            side_out[e * rows : (e + 1) * rows],
            side_in_ref[pl.ds(e * rows, rows), :],
            (((0,), (0,)), ((), ())),
            preferred_element_type=jnp.float32,
        ).astype(jnp.bfloat16)


def stage_kernel(queries_ref, out_ref, sem):
    copy = pltpu.make_async_copy(queries_ref, out_ref, sem)
    copy.start()
    copy.wait()


def staged(queries):
    return pl.pallas_call(
        stage_kernel,
        out_shape=pltpu.VMEM(queries.shape, queries.dtype),
        in_specs=[pl.BlockSpec(memory_space=pl.ANY)],
        out_specs=pl.BlockSpec(memory_space=pltpu.VMEM),
        scratch_shapes=[pltpu.SemaphoreType.DMA],
        compiler_params=pltpu.CompilerParams(vmem_limit_bytes=8 * 1024 * 1024),
        name="stage",
    )(queries)


def raw_kernel(place_ref, grads_ref, queries_ref, out_ref):
    chips, _, lanes = out_ref.shape
    share = queries_ref.shape[0] // chips
    grads = grads_ref[...]
    raw = lax.dot_general(
        grads, queries_ref[...], (((1,), (1,)), ((), ())), preferred_element_type=jnp.float32
    )
    wide = grads.astype(jnp.float32)
    squares = jnp.sum(wide * wide, axis=1, keepdims=True)
    fill = jnp.broadcast_to(squares, (grads.shape[0], lanes - share))
    for slot in range(chips):
        origin = (place_ref[0] + chips - slot) % chips
        out_ref[origin] = jnp.concatenate([raw[:, slot * share : (slot + 1) * share], fill], axis=1)


def fold_kernel(parts_ref, out_ref, *, share):
    chips, per = parts_ref.shape[:2]
    each = 8 // per
    raws, squares = [], []
    for j in range(chips // each):
        rows = jnp.concatenate([parts_ref[j * each + k] for k in range(each)], axis=0)
        raws.append(rows[:, :share])
        squares.append(rows[:, share : 2 * share])
    block = jnp.concatenate([jnp.concatenate(raws, axis=1), jnp.concatenate(squares, axis=1)], axis=0)
    for s in range(out_ref.shape[0]):
        out_ref[s] = block


def scores_kernel(parts_ref, out_ref, *, count):
    total = parts_ref[0]
    for s in range(1, parts_ref.shape[0]):
        total = total + parts_ref[s]
    scores = total[:8] / jnp.sqrt(total[8:] / count + 1e-06)
    share = out_ref.shape[1]
    for j in range(out_ref.shape[0] // 8):
        out_ref[pl.ds(8 * j, 8), :] = scores[:, j * share : (j + 1) * share]


def to_tiles(rows):
    count, width = rows.shape
    tiles = rows.reshape(count // 8, 8, width // LANES, LANES).transpose(0, 2, 1, 3)
    return tiles.reshape(count // 8, width // (2 * LANES), SUBLANES, LANES)


def from_tiles(tiles):
    groups, blocks = tiles.shape[:2]
    rows = tiles.reshape(groups, blocks * 2, 8, LANES).transpose(0, 2, 1, 3)
    return rows.reshape(groups * 8, blocks * 2 * LANES)


def chain_back(grad_rows, resid_rows, norm_gain):
    grad_f32 = grad_rows.astype(jnp.float32)
    resid_f32 = resid_rows.astype(jnp.float32)
    inv_rms = lax.rsqrt(jnp.mean(resid_f32 * resid_f32, axis=-1, keepdims=True) + EPS)
    weighted = grad_f32 * norm_gain
    inner_mean = jnp.mean(weighted * resid_f32, axis=-1, keepdims=True)
    result = grad_f32 + inv_rms * weighted - resid_f32 * (inv_rms * inv_rms * inv_rms) * inner_mean
    return result.astype(jnp.bfloat16)


def shards(hidden_acts, resid_stream, norm_scale, out_grad, lengths, proj_in, proj_out, queries):
    tok_rows, features = out_grad.shape
    examples = lengths.shape[0]
    seq_len = tok_rows // examples
    rank_size = proj_in.shape[1]
    sections = lax.axis_size("section")
    ranks = lax.axis_size("dp")
    share = queries.shape[1]
    me = lax.axis_index("section")
    resid_rows = resid_stream[0]
    norm_gain = norm_scale[0]

    side = math.isqrt(sections)
    grid = [(row, column) for row in range(side) for column in range(side)]

    def moved(value, down, across):
        pairs = [
            (row * side + column, (row + down) % side * side + (column + across) % side) for row, column in grid
        ]
        return lax.ppermute(value, "section", pairs)

    gain_tiles = norm_gain.reshape(-1, LANES)
    across = [moved(gain_tiles, 0, k) for k in range(1, side)]
    resid_first = resid_rows
    near = [jnp.stack([gain_tiles] + across)]
    near[0], own_queries = lax.optimization_barrier((near[0], queries[0]))
    near += [moved(near[0], k, 0) for k in range(1, side)]

    side_in = jnp.einsum(
        "tf,rf->tr", hidden_acts[0], proj_in[0], preferred_element_type=jnp.float32
    ).astype(jnp.bfloat16)

    chips = ranks // 2

    def around(value, steps):
        return lax.ppermute(value, "dp", [(i, (i + 2 * steps) % ranks) for i in range(ranks)])

    def longer(ring, steps, count):
        for _ in range(count):
            ring.append(around(ring[-1], steps))

    up, down = [own_queries], [own_queries]
    longer(up, 1, 1)
    longer(down, -1, 1)

    own = tok_rows // sections
    recv = lax.all_to_all(to_tiles(resid_first), "section", 0, 0)
    recv, side_in, up, down = lax.optimization_barrier((recv, side_in, up, down))
    longer(up, 1, chips // 2 - 1)
    longer(down, -1, chips - 2 - chips // 2)
    all_queries = jnp.concatenate(up + down[:0:-1])
    own_rows = lax.dynamic_slice_in_dim(out_grad, me * own, own, axis=0)
    own_slots = me * own + jnp.arange(own, dtype=jnp.int32)
    own_live = own_slots % seq_len < jnp.take(lengths, own_slots // seq_len)
    own_top = jnp.where(own_live[:, None], own_rows, jnp.zeros_like(own_rows))
    grads = chain_all(me.astype(jnp.int32).reshape(1), recv, to_tiles(own_top)[0], near)
    held, all_queries = lax.optimization_barrier((lax.all_to_all(grads, "section", 0, 0), all_queries))
    held_grad = from_tiles(held)

    outer = in_vmem(front_kernel, jax.ShapeDtypeStruct((examples, rank_size, rank_size), jnp.bfloat16), "front")(
        held_grad, proj_out[0], side_in
    )
    example_grads = outer.reshape(examples, rank_size * rank_size)
    example_grads, all_queries = lax.optimization_barrier((example_grads, all_queries))
    all_queries = staged(all_queries)
    rank = lax.axis_index("dp")
    other_grads = lax.ppermute(example_grads, "dp", [(i, i ^ 1) for i in range(ranks)])
    first, second = (jnp.where(rank % 2 == k, example_grads, other_grads) for k in range(2))
    raw = in_vmem(
        raw_kernel,
        jax.ShapeDtypeStruct((chips, 2 * examples, LANES), jnp.float32),
        "raw",
        scalars=1,
    )((rank // 2).astype(jnp.int32).reshape(1), jnp.concatenate([first, second]), all_queries)
    held_grad, raw = lax.optimization_barrier((held_grad, raw))
    in_grad = chain_back(held_grad, resid_rows, norm_gain)
    same_core = [list(range(core, ranks, 2)) for core in range(2)]
    raw = lax.all_to_all(raw, "dp", 0, 0, axis_index_groups=same_core)
    folded = in_vmem(
        functools.partial(fold_kernel, share=queries.shape[1]),
        jax.ShapeDtypeStruct((sections, 16, LANES), jnp.float32),
        "fold",
    )(raw)
    parts = lax.all_to_all(folded, "section", 0, 0)
    scores = in_vmem(
        functools.partial(scores_kernel, count=sections * rank_size * rank_size),
        jax.ShapeDtypeStruct((ranks * examples, share), jnp.float32),
        "scores",
    )(parts)
    return (scores, in_grad[None])


def solution(mesh):
    in_specs = (
        P("section", "dp", None),
        P("section", "dp", None),
        P("section", None),
        P("dp", None),
        P("dp"),
        P("section", None, None),
        P("section", None, None),
        P("section", "dp", None),
    )
    out_specs = (P(None, "dp"), P("section", "dp", None))
    return jax.shard_map(shards, mesh=mesh, in_specs=in_specs, out_specs=out_specs, check_vma=False)
```
